32 devices in a mesh: wide: 16 (over z, y, x), narrow: 2 (over core).
Axes of the slice: x: 2, y: 2, z: 4, core: 2. Of those that a mesh axis runs over, the one named last changes fastest.
Arguments:
- user_table: bfloat16 [65536, 256], P('wide'), may hold values from -3 to 3
- item_table: bfloat16 [32768, 256], P('wide'), may hold values from -3 to 3
- week_table: bfloat16 [1024, 256], P('wide'), may hold values from -3 to 3
- profile: bfloat16 [65536, 4096], P('wide', 'narrow'), may hold values from -6 to 6
- feature_table: bfloat16 [4096, 256], P('narrow'), may hold values from -0.375 to 0.375
- user_req: int32 [32, 16, 32], P(('wide', 'narrow')), may hold values from 0 to 4095
- item_req: int32 [32, 16, 32], P(('wide', 'narrow')), may hold values from 0 to 2047
- week_req: int32 [32, 16, 4], P(('wide', 'narrow')), may hold values from 0 to 63
- user_counts: int32 [32, 16], P(('wide', 'narrow')), may hold values from 1 to 32, 256 in all within a row
- item_counts: int32 [32, 16], P(('wide', 'narrow')), may hold values from 1 to 32, 256 in all within a row
- week_counts: int32 [32, 16], P(('wide', 'narrow')), may hold values from 1 to 4, 28 in all within a row
- pos_cells: int32 [32, 4096], P(('wide', 'narrow')), may hold values from 0 to 1835007
Outputs:
- grad_users: float32 [65536, 256], P(('wide', 'narrow'))
- grad_items: float32 [32768, 256], P(('wide', 'narrow'))
- grad_weeks: float32 [1024, 256], P(('wide', 'narrow'))
- grad_features: float32 [4096, 256], P('narrow')
The draws below stay inside these ranges and needn't reach their ends.
Inputs may be any that keep to these rules, and one draw needn't show every extreme that they name: `user_req`: only the first user_counts[d, o] slots of owner o are read; the rest hold arbitrary row numbers. Rows may repeat. `item_req`: only the first item_counts[d, o] slots of owner o are read. `week_req`: only the first week_counts[d, o] slots of owner o are read. `user_counts`: each block's counts sum to 256; every block has an owner with exactly 32. `item_counts`: each block's counts sum to 256; every block has an owner with exactly 32. `week_counts`: each block's counts sum to 28; every block has an owner with exactly 4. `pos_cells`: cells may repeat.
All inputs are finite; a program needn't handle non-finite values.
Results may differ from the reference program's by a relative error of at most 0.0015.
Values may be sent and summed in bfloat16 or wider, within the bound.
No kernel may reach another device: no remote copies, remote signals or barrier semaphores. Data moves between devices by JAX's collectives and lax.ppermute only.
A program may use at most 128 MiB of HBM per device.

```python
import math
import jax
import jax.numpy as jnp
import numpy as np
from jax import lax

RANK = 256
FEAT = 4096
BU = 256
BI = 256
BW = 28
CAPU = 32
CAPI = 32
CAPW = 4
NPOS = 4096
UR_DEV = 4096
IR_DEV = 2048
WR_DEV = 64
USERS = 65536
ITEMS = 32768
WEEKS = 1024
N_WIDE = 16
DEVICES = 32


def place_ends(values, own_key, smallest, high):
    spot = [jax.random.randint(jax.random.fold_in(own_key, axis), (), 0, length) for axis, length in enumerate(values.shape)]
    widest = values.shape.index(max(values.shape))
    neighbour = spot[:widest] + [(spot[widest] + 1) % values.shape[widest]] + spot[widest + 1:]
    return values.at[tuple(spot)].set(smallest).at[tuple(neighbour)].set(high)


def levels(own_key, shape, pieces, least, high):
    def one(position, blocks):
        steps = jax.random.uniform(jax.random.fold_in(jax.random.fold_in(own_key, 6), position), (blocks,), jnp.float32, least / len(pieces), high / len(pieces))
        return jnp.repeat(jnp.exp(steps), shape[position] // blocks).reshape((-1,) + (1,) * (len(shape) - position - 1))

    gain = one(*pieces[0])
    for cut in pieces[1:]:
        gain = gain * one(*cut)
    return gain


def length_profile(amount, total, limit, slope):
    portions = [(1 << 20) // math.isqrt(grade ** slope) + 1 for grade in range(2, amount + 1)]
    spare, given = total - limit - (amount - 1), [1] * (amount - 1)
    while spare > 0:
        candidates = [i for i in range(amount - 1) if given[i] < limit]
        mass, budget = sum([portions[i] for i in candidates]), spare
        for i in candidates:
            extra = min(limit - given[i], max(1, budget * portions[i] // mass), spare)
            given[i] = given[i] + extra
            spare = spare - extra
    return np.array([limit] + given)


def ragged_sizes(own_key, number_of, total, limit, skew):
    if number_of == 2:
        one = jax.random.randint(own_key, (), max(1, total - limit), min(limit, total - 1) + 1)
        return jnp.stack([one, total - one])
    lengths = jnp.asarray(length_profile(number_of, total, limit, skew), jnp.int32)
    pairs = (number_of - 1) // 2
    giver, taker = lengths[1:1 + 2 * pairs:2], lengths[2:2 + 2 * pairs:2]
    margin = jnp.minimum(giver - 1, limit - taker)
    moved = jax.random.randint(jax.random.fold_in(own_key, 1), (pairs,), 0, 1 << 20) % (margin + 1)
    lengths = lengths.at[1:1 + 2 * pairs:2].set(giver - moved).at[2:2 + 2 * pairs:2].set(taker + moved)
    return lengths[jax.random.permutation(jax.random.fold_in(own_key, 2), number_of)]


def centred(key, shape, deviation, most, split=(), held_as=jnp.bfloat16):
    drawn = deviation * jax.random.normal(key, shape, jnp.float32)
    if split:
        drawn = drawn * levels(key, shape, split, -0.22, 0.18)
    return jnp.clip(drawn, -most, most).astype(held_as)


def setup_inputs(seed: int = 0) -> dict:
    splits = jax.random.split(jax.random.key(seed), 13)
    user_table = centred(splits[0], (USERS, RANK), 0.5, 3.0, ((0, 16),))
    item_table = centred(splits[1], (ITEMS, RANK), 0.5, 3.0, ((0, 16),))
    week_table = centred(splits[2], (WEEKS, RANK), 0.5, 3.0, ((0, 16),))
    profile = centred(splits[3], (USERS, FEAT), 1.0, 6.0, ((0, 16), (1, 2)))
    feature_table = centred(splits[4], (FEAT, RANK), 0.0625, 0.375, ((0, 2),))
    user_req = place_ends(jax.random.randint(splits[5], (DEVICES, N_WIDE, CAPU), 0, UR_DEV), jax.random.fold_in(splits[5], 1), 0, UR_DEV - 1).astype(jnp.int32)
    item_req = place_ends(jax.random.randint(splits[6], (DEVICES, N_WIDE, CAPI), 0, IR_DEV), jax.random.fold_in(splits[6], 1), 0, IR_DEV - 1).astype(jnp.int32)
    week_req = place_ends(jax.random.randint(splits[7], (DEVICES, N_WIDE, CAPW), 0, WR_DEV), jax.random.fold_in(splits[7], 1), 0, WR_DEV - 1).astype(jnp.int32)
    user_counts = jax.vmap(lambda own: ragged_sizes(own, N_WIDE, BU, CAPU, 1))(jax.random.split(splits[8], DEVICES)).reshape((DEVICES, N_WIDE)).astype(jnp.int32)
    item_counts = jax.vmap(lambda own: ragged_sizes(own, N_WIDE, BI, CAPI, 1))(jax.random.split(splits[9], DEVICES)).reshape((DEVICES, N_WIDE)).astype(jnp.int32)
    week_counts = jax.vmap(lambda own: ragged_sizes(own, N_WIDE, BW, CAPW, 1))(jax.random.split(splits[10], DEVICES)).reshape((DEVICES, N_WIDE)).astype(jnp.int32)
    pos_cells = place_ends(jax.random.randint(splits[11], (DEVICES, NPOS), 0, BW * BU * BI), jax.random.fold_in(splits[11], 1), 0, (BW * BU * BI) - 1).astype(jnp.int32)
    return {"user_table": user_table, "item_table": item_table, "week_table": week_table, "profile": profile, "feature_table": feature_table, "user_req": user_req, "item_req": item_req, "week_req": week_req, "user_counts": user_counts, "item_counts": item_counts, "week_counts": week_counts, "pos_cells": pos_cells}


def compact_index(counts, cap, total):
    ends = jnp.cumsum(counts).astype(jnp.int32)
    starts = ends - counts
    place = jnp.arange(total, dtype=jnp.int32)
    owner = jnp.sum((ends[None, :] <= place[:, None]).astype(jnp.int32), axis=1)
    onehot = (owner[:, None] == jnp.arange(counts.shape[0], dtype=jnp.int32)[None, :]).astype(jnp.int32)
    first = jnp.sum(onehot * starts[None, :], axis=1)
    return (owner * cap + place - first).astype(jnp.int32)


def block_grads(user_rows, item_rows, week_rows, pos):
    nweek, nuser, nitem = week_rows.shape[0], user_rows.shape[0], item_rows.shape[0]
    user_f = user_rows.astype(jnp.float32)
    week_f = week_rows.astype(jnp.float32)
    item_f = item_rows.astype(jnp.float32)
    mixed = (user_f[None] * week_f[:, None]).astype(jnp.bfloat16)
    mixed_f = mixed.astype(jnp.float32)
    model = jnp.einsum("kir,jr->kij", mixed_f, item_f)
    cells = nweek * nuser * nitem
    cpos = jnp.zeros((cells,), jnp.float32).at[pos].set(1.0).reshape(nweek, nuser, nitem)
    resid = (jax.nn.sigmoid(model) - cpos).astype(jnp.bfloat16).astype(jnp.float32)
    partial_value = jnp.einsum("kij,jr->kir", resid, item_f)
    grad_u = jnp.sum(partial_value * week_f[:, None, :], axis=0)
    grad_w = jnp.sum(partial_value * user_f[None], axis=1)
    grad_v = jnp.einsum("kij,kir->jr", resid, mixed_f)
    return grad_u, grad_v, grad_w


def reference(user_table, item_table, week_table, profile, feature_table, user_req, item_req, week_req, user_counts, item_counts, week_counts, pos_cells):
    owners = jnp.arange(N_WIDE, dtype=jnp.int32)[:, None]

    def one_block(carry, device):
        acc_u, acc_v, acc_w = carry
        glob_u = (owners * UR_DEV + user_req[device]).reshape(-1)[compact_index(user_counts[device], CAPU, BU)]
        glob_v = (owners * IR_DEV + item_req[device]).reshape(-1)[compact_index(item_counts[device], CAPI, BI)]
        glob_w = (owners * WR_DEV + week_req[device]).reshape(-1)[compact_index(week_counts[device], CAPW, BW)]
        grad_u, grad_v, grad_w = block_grads(user_table[glob_u], item_table[glob_v], week_table[glob_w], pos_cells[device])
        return (acc_u.at[glob_u].add(grad_u), acc_v.at[glob_v].add(grad_v), acc_w.at[glob_w].add(grad_w)), None

    start = (jnp.zeros((USERS, RANK), jnp.float32), jnp.zeros((ITEMS, RANK), jnp.float32), jnp.zeros((WEEKS, RANK), jnp.float32))
    (acc_u, acc_v, acc_w), _ = lax.scan(one_block, start, jnp.arange(DEVICES, dtype=jnp.int32))

    slabs_u = user_table.reshape(N_WIDE, UR_DEV, RANK)
    slabs_x = profile.reshape(N_WIDE, UR_DEV, FEAT)

    def one_slab(acc_h, pair):
        slab_u, slab_x = pair
        model = jnp.dot(slab_u, feature_table.T, preferred_element_type=jnp.float32)
        resid = (model - slab_x.astype(jnp.float32)).astype(jnp.bfloat16)
        grad_u = 0.0625 * jnp.dot(resid, feature_table, preferred_element_type=jnp.float32)
        grad_h = 0.0625 * jnp.dot(resid.T, slab_u, preferred_element_type=jnp.float32)
        return acc_h + grad_h, grad_u

    grad_h, prof_u = lax.scan(one_slab, jnp.zeros((FEAT, RANK), jnp.float32), (slabs_u, slabs_x))
    grad_users = acc_u + prof_u.reshape(USERS, RANK)
    return grad_users, acc_v, acc_w, grad_h
```

```python
import functools

import jax
import jax.numpy as jnp
from jax import lax
from jax.experimental import pallas as pl
from jax.experimental.pallas import tpu as pltpu
from jax.sharding import PartitionSpec as P

RANK = 256
BU = 256
BI = 256
BW = 28
BWP = 32
CAPU = 32
CAPI = 32
CAPW = 4
SLOT = 80
TAIL = 16
HALF = 14
F32, BF16, I32, I16 = jnp.float32, jnp.bfloat16, jnp.int32, jnp.int16
NN = (((1,), (0,)), ((), ()))
NT = (((1,), (1,)), ((), ()))
TN = (((0,), (0,)), ((), ()))


def mm(a, b, dims=NN):
    return lax.dot_general(a, b, dims, preferred_element_type=F32)


def iota(shape, dim):
    return lax.broadcasted_iota(I32, shape, dim)


def params(**kw):
    return pltpu.CompilerParams(vmem_limit_bytes=56 << 20, **kw)


def cost(flops, nbytes):
    return pl.CostEstimate(flops=flops, bytes_accessed=nbytes, transcendentals=0)


VM = pl.BlockSpec(memory_space=pltpu.VMEM)
SM = pl.BlockSpec(memory_space=pltpu.SMEM)


def pow2(e):
    return jnp.exp2(e).astype(BF16).astype(F32)


def row_exponent(g):
    m = jnp.max(jnp.abs(g), axis=1, keepdims=True)
    return jnp.clip(jnp.ceil(jnp.log2(jnp.maximum(m, 1e-30))), -96.0, 110.0)


def column_of(row):
    return jnp.broadcast_to(row, (128, 128)).T[:, :1]


def gather_kernel(owners, got_ref, ut_ref, it_ref, wt_ref, out_ref):
    got = got_ref[...]
    flip = jnp.concatenate([got, jnp.zeros((128 - owners, 128), I32)], axis=0).T

    def pick(first, count, table_ref, step):
        col = jnp.concatenate([flip[first : first + count, w : w + 1] for w in range(owners)], axis=0)
        rows = table_ref.shape[0]
        acc = None
        for c in range(0, rows, step):
            hit = iota((owners * count, step), 1) == col - c
            part = mm(jnp.where(hit, 1.0, 0.0).astype(BF16), table_ref[c : c + step, :])
            acc = part if acc is None else acc + part
        return acc.astype(BF16)

    u = pick(0, CAPU, ut_ref, 512)
    v = pick(CAPU, CAPI, it_ref, 512)
    w = pick(CAPU + CAPI, TAIL, wt_ref, wt_ref.shape[0])
    for o in range(owners):
        b = SLOT * o
        out_ref[b : b + CAPU, :] = u[CAPU * o : CAPU * (o + 1)]
        out_ref[b + CAPU : b + CAPU + CAPI, :] = v[CAPI * o : CAPI * (o + 1)]
        out_ref[b + CAPU + CAPI : b + SLOT, :] = w[TAIL * o : TAIL * (o + 1)]


def gather_rows(got, ut, it, wt):
    owners = got.shape[0]
    return pl.pallas_call(
        functools.partial(gather_kernel, owners),
        in_specs=[VM] * 4,
        out_specs=VM,
        out_shape=jax.ShapeDtypeStruct((owners * SLOT, RANK), BF16),
        compiler_params=params(),
        cost_estimate=cost(2 << 30, 4 << 20),
        name="gather_rows",
    )(got, ut, it, wt)


def positives_kernel(p_ref, out_ref):
    n = p_ref.shape[0]
    rows = [p_ref[c : c + 1, :] for c in range(n)]
    near = [None] * n
    for a in range(n):
        col = jnp.broadcast_to(rows[a], (128, 128)).T
        for c in range(a, n):
            x = col ^ rows[c]
            if c == a:
                x = jnp.where(iota((128, 128), 0) < iota((128, 128), 1), x, 1)
            best = x[0:8]
            for s in range(8, 128, 8):
                best = jnp.minimum(best, x[s : s + 8])
            near[c] = best if near[c] is None else jnp.minimum(near[c], best)
    lo = hi = None
    group = 4
    for g in range(0, n, group):
        pos = jnp.concatenate(rows[g : g + group], axis=1)
        first = jnp.concatenate([jnp.min(near[c], axis=0, keepdims=True) for c in range(g, g + group)], axis=1)
        week = pos >> 16
        bit = jnp.where(first == 0, 0, 1)
        low = jnp.where(week < HALF, bit << week, 0).astype(F32)
        high = jnp.where(week < HALF, 0, bit << jnp.maximum(week - HALF, 0)).astype(F32)
        user_hit = iota((BU, group * 128), 0) == (pos >> 8) & (BU - 1)
        item_hit = iota((BI, group * 128), 0) == pos & (BI - 1)
        item = jnp.where(item_hit, 1.0, 0.0).astype(BF16)
        part_lo = mm(jnp.where(user_hit, low, 0.0).astype(BF16), item, NT)
        part_hi = mm(jnp.where(user_hit, high, 0.0).astype(BF16), item, NT)
        lo = part_lo if lo is None else lo + part_lo
        hi = part_hi if hi is None else hi + part_hi
    out_ref[...] = lo.astype(I32) | (hi.astype(I32) << HALF)


def positives(pos):
    return pl.pallas_call(
        positives_kernel,
        in_specs=[VM],
        out_specs=VM,
        out_shape=jax.ShapeDtypeStruct((BU, BI), I32),
        compiler_params=params(),
        cost_estimate=cost(4 << 30, 1 << 20),
        name="positives",
    )(pos.reshape(-1, 128))


def block_kernel(owners, back_ref, bits_ref, uc_ref, vc_ref, wc_ref, out_ref, gu, gvt, gw):
    def listed(count_ref, cap, stride, first, total):
        slots = owners * stride
        lane = iota((1, slots), 1)
        place = jnp.full((1, slots), -1, I32)
        start = 0
        back = []
        for o in range(owners):
            n = count_ref[0, o]
            s = lane - stride * o
            place = jnp.where((s >= 0) & (s < n), start + s, place)
            sub = iota((stride, total), 0)
            hit = (iota((stride, total), 1) == sub + start) & (sub < n)
            back.append(jnp.where(hit, 1.0, 0.0))
            start = start + n
        hit = iota((total, slots), 0) == place
        got = jnp.concatenate(
            [back_ref[SLOT * o + first : SLOT * o + first + stride, :] for o in range(owners)], axis=0
        )
        rows = mm(jnp.where(hit, 1.0, 0.0).astype(BF16), got)
        return rows, hit, jnp.concatenate(back, axis=0).astype(BF16)

    u, hit_u, into_u = listed(uc_ref, CAPU, CAPU, 0, BU)
    v, hit_v, into_v = listed(vc_ref, CAPI, CAPI, CAPU, BI)
    w, hit_w, into_w = listed(wc_ref, CAPW, TAIL, CAPU + CAPI, BWP)
    vb = v.astype(BF16)
    ut = u.T
    wt = jnp.concatenate([w, jnp.zeros((128 - BWP, RANK), F32)], axis=0).T
    gw[...] = jnp.zeros_like(gw)
    bits = bits_ref
    for k in range(BW):
        wk = w[k : k + 1, :]
        uw = (u * wk).astype(BF16)
        m = mm(uw, vb, NT)
        pos = ((bits[...] >> k) & 1).astype(F32)
        g = (1.0 / (1.0 + jnp.exp(-m)) - pos).astype(BF16)
        q = mm(g, vb)
        uwt = (ut * wt[:, k : k + 1]).astype(BF16)
        pv = mm(uwt, g)
        if k == 0:
            gu[...] = q * wk
            gvt[...] = pv
        else:
            gu[...] += q * wk
            gvt[...] += pv
        gw[k : k + 1, :] = jnp.sum(q * u, axis=0, keepdims=True)

    def slots_of(g, hit, into):
        e = row_exponent(g)
        q = jnp.round(g * pow2(14.0 - e))
        hi = jnp.round(q * (1.0 / 256.0))
        lo = q - 256.0 * hi
        placed = 256.0 * mm(into, hi.astype(BF16)) + mm(into, lo.astype(BF16))
        row = jnp.sum(jnp.where(hit, e, 0.0), axis=0, keepdims=True)
        return placed, row

    qu, eu = slots_of(gu[...], hit_u, into_u)
    qv, ev = slots_of(gvt[...].T, hit_v, into_v)
    qw, ew = slots_of(gw[...], hit_w, into_w)
    lane = iota((8, 128), 1)

    def to_lane(row, width, o, lane_at):
        per = 128 // width
        cut = jnp.broadcast_to(row[:, 128 * (o // per) : 128 * (o // per + 1)], (8, 128))
        return pltpu.roll(cut, (lane_at - width * (o % per)) % 128, 1)

    sub = iota((TAIL, RANK), 0)
    for o in range(owners):
        b = SLOT * o
        out_ref[b : b + CAPU, :] = qu[CAPU * o : CAPU * (o + 1)].astype(I32).astype(I16)
        out_ref[b + CAPU : b + CAPU + CAPI, :] = qv[CAPI * o : CAPI * (o + 1)].astype(I32).astype(I16)
        exps = jnp.where(
            lane < CAPU,
            to_lane(eu, CAPU, o, 0),
            jnp.where(lane < CAPU + CAPI, to_lane(ev, CAPI, o, CAPU), to_lane(ew, TAIL, o, CAPU + CAPI)),
        )
        exps = jnp.concatenate([exps[0:1], exps[0:1]], axis=1)
        tail = jnp.where(sub == 8, exps, jnp.where(sub < CAPW, qw[TAIL * o : TAIL * (o + 1)], 0.0))
        out_ref[b + CAPU + CAPI : b + SLOT, :] = tail.astype(I32).astype(I16)


def block_slots(back, bits, uc, vc, wc):
    owners = uc.shape[1]
    return pl.pallas_call(
        functools.partial(block_kernel, owners),
        in_specs=[VM, VM, SM, SM, SM],
        out_specs=VM,
        out_shape=jax.ShapeDtypeStruct((owners * SLOT, RANK), I16),
        scratch_shapes=[pltpu.VMEM((BU, RANK), F32), pltpu.VMEM((RANK, BI), F32), pltpu.VMEM((BWP, RANK), F32)],
        compiler_params=params(),
        cost_estimate=cost(4 << 30, 2 << 20),
        name="block_slots",
    )(back, bits, uc, vc, wc)


def dense_kernel(shares, per, chunk, n_ref, x_ref, u_ref, f_ref, others_ref, mine_ref, gf_ref, acc):
    t = pl.program_id(0)
    u = u_ref[...]
    nf = f_ref.shape[0]

    @pl.when(t == 0)
    def _():
        acc[...] = jnp.zeros_like(acc)

    total = None
    for c in range(0, nf, chunk):
        f = f_ref[c : c + chunk, :]
        r = (mm(u, f, NT) - x_ref[:, c : c + chunk].astype(F32)).astype(BF16)
        part = mm(r, f)
        total = part if total is None else total + part
        acc[c : c + chunk, :] += mm(r, u, TN)

    @pl.when(t < (shares - 1) * per)
    def _():
        others_ref[...] = 0.0625 * total

    @pl.when(t >= (shares - 1) * per)
    def _():
        mine_ref[...] = 0.0625 * total

    @pl.when(t == pl.num_programs(0) - 1)
    def _():
        pack_features(0.0625 * acc[...], gf_ref)


def pack_features(g, out_ref):
    nf = g.shape[0]
    c = nf // 16
    eye = iota((c, 128), 0) == iota((c, 128), 1)
    for o in range(16):
        part = g[c * o : c * (o + 1)]
        e = row_exponent(part)
        q = jnp.round(part * pow2(14.0 - e))
        row = jnp.sum(jnp.where(eye, e, 0.0), axis=0, keepdims=True)
        row = jnp.concatenate([row, row], axis=1)
        b = (c + TAIL) * o
        out_ref[b : b + c, :] = q.astype(I32).astype(I16)
        tail = jnp.where(iota((TAIL, RANK), 0) == 8, row, 0.0)
        out_ref[b + c : b + c + TAIL, :] = tail.astype(I32).astype(I16)


def dense(n, x, u, f, shares):
    nu, nf = x.shape
    own = nu // shares
    tile = 512
    per = own // tile
    tiles = nu // tile

    def rows(t, n_ref):
        return (lax.rem(n_ref[0] + 1 + t // per, shares) * per + lax.rem(t, per), 0)

    return pl.pallas_call(
        functools.partial(dense_kernel, shares, per, nf),
        grid_spec=pltpu.PrefetchScalarGridSpec(
            num_scalar_prefetch=1,
            grid=(tiles,),
            in_specs=[
                pl.BlockSpec((tile, nf), rows),
                pl.BlockSpec((tile, RANK), rows),
                pl.BlockSpec((nf, RANK), lambda t, n_ref: (0, 0)),
            ],
            out_specs=[
                pl.BlockSpec((tile, RANK), lambda t, n_ref: (jnp.minimum(t, (shares - 1) * per - 1), 0)),
                pl.BlockSpec((tile, RANK), lambda t, n_ref: (jnp.maximum(t - (shares - 1) * per, 0), 0)),
                pl.BlockSpec((nf + 16 * TAIL, RANK), lambda t, n_ref: (0, 0)),
            ],
            scratch_shapes=[pltpu.VMEM((nf, RANK), F32)],
        ),
        out_shape=[
            jax.ShapeDtypeStruct(((shares - 1) * own, RANK), F32),
            jax.ShapeDtypeStruct((own, RANK), F32),
            jax.ShapeDtypeStruct((nf + 16 * TAIL, RANK), I16),
        ],
        compiler_params=params(dimension_semantics=("arbitrary",)),
        cost_estimate=cost(3 * 2 * nu * nf * RANK, 2 * nu * nf + 8 * nu * RANK),
        name="dense",
    )(n, x, u, f)


def unpacked(block, c):
    q = block[:c].astype(I32).astype(F32)
    e = block[c : c + TAIL].astype(I32).astype(F32)[8:9, :128]
    return q * pow2(column_of(e)[:c] - 14.0)


def sum_kernel(c, in_ref, a_ref, b_ref):
    total = None
    for o in range(16):
        part = unpacked(in_ref[(c + TAIL) * o : (c + TAIL) * (o + 1), :], c)
        total = part if total is None else total + part
    e = row_exponent(total)
    q = jnp.round(total * pow2(14.0 - e)).astype(I32)
    eye = iota((c, 128), 0) == iota((c, 128), 1)
    row = jnp.sum(jnp.where(eye, e, 0.0), axis=0, keepdims=True)
    tail = jnp.where(iota((TAIL, 128), 0) == 8, row, 0.0)
    a_ref[:c, :] = q[:, :128].astype(I16)
    a_ref[c:, :] = tail.astype(I32).astype(I16)
    b_ref[...] = q[:, 128:].astype(I16)


def sum_features(parts, c):
    return pl.pallas_call(
        functools.partial(sum_kernel, c),
        in_specs=[VM],
        out_specs=[VM, VM],
        out_shape=[jax.ShapeDtypeStruct((c + TAIL, 128), I16), jax.ShapeDtypeStruct((c, 128), I16)],
        compiler_params=params(),
        cost_estimate=cost(1 << 20, 2 << 20),
        name="sum_features",
    )(parts)


ORDER_A = (8, 4, 2, 1)
ORDER_B = (8, 4, 1, 2)


def spread(x, order):
    for bit in order:
        x = jnp.concatenate([x, lax.ppermute(x, "wide", [(i, i ^ bit) for i in range(16)])], axis=0)
    return x


def flips(order):
    out = []
    for j in range(16):
        out.append(sum(bit for i, bit in enumerate(order) if (j >> i) & 1))
    return out


def decode_kernel(c, w_ref, a_ref, b_ref, out_ref):
    me = w_ref[0]
    at_b = flips(ORDER_B)
    for j, flip in enumerate(flips(ORDER_A)):
        i = at_b.index(flip)
        base = (c + TAIL) * j
        e = a_ref[base + c : base + c + TAIL, :].astype(I32).astype(F32)[8:9, :]
        scale = pow2(column_of(e)[:c] - 14.0)
        at = pl.multiple_of((me ^ flip) * c, c)
        out_ref[pl.ds(at, c), :128] = a_ref[base : base + c, :].astype(I32).astype(F32) * scale
        out_ref[pl.ds(at, c), 128:] = b_ref[c * i : c * (i + 1), :].astype(I32).astype(F32) * scale


def decode_features(w, a, b, c):
    return pl.pallas_call(
        functools.partial(decode_kernel, c),
        in_specs=[SM, VM, VM],
        out_specs=VM,
        out_shape=jax.ShapeDtypeStruct((16 * c, RANK), F32),
        compiler_params=params(),
        cost_estimate=cost(1 << 20, 3 << 20),
        name="decode_features",
    )(w, a, b)


def lanes(x, width, off):
    per = 128 // width
    rolled = [pltpu.roll(x, (width * j - off) % 128, 1) for j in range(per)]
    lane = iota((1, 128), 1) // width
    out = []
    for g in range(16 // per):
        acc = rolled[0][per * g : per * g + 1, :]
        for j in range(1, per):
            acc = jnp.where(lane == j, rolled[j][per * g + j : per * g + j + 1, :], acc)
        out.append(acc)
    return jnp.concatenate(out, axis=1)


def owner_kernel(shares, n_ref, *refs):
    gots, rets = refs[:shares], refs[shares : 2 * shares]
    parts = refs[2 * shares : 3 * shares]
    users_ref, items_ref, weeks_ref = refs[3 * shares :]
    n = n_ref[0]
    kinds = []
    for got_ref, ret_ref in zip(gots, rets):
        got = got_ref[...]
        tails = [
            ret_ref[SLOT * o + CAPU + CAPI : SLOT * (o + 1), :].astype(I32).astype(F32) for o in range(16)
        ]
        exps = jnp.concatenate([t[8:9, :128] for t in tails], axis=0)
        scale = pow2(exps - 14.0)

        def split(q):
            hi = jnp.round(q * (1.0 / 256.0))
            return hi.astype(BF16), (q - 256.0 * hi).astype(BF16)

        def rows(first, count):
            return jnp.concatenate(
                [ret_ref[SLOT * o + first : SLOT * o + first + count, :] for o in range(16)], axis=0
            ).astype(I32).astype(F32)

        tail_ok = iota((1, 16 * TAIL), 1) % TAIL < CAPW
        wk = jnp.where(tail_ok, lanes(got, TAIL, CAPU + CAPI), -1)
        kinds.append(
            (
                (lanes(got, CAPU, 0), lanes(scale, CAPU, 0), split(rows(0, CAPU))),
                (lanes(got, CAPI, CAPU), lanes(scale, CAPI, CAPU), split(rows(CAPU, CAPI))),
                (wk, lanes(scale, TAIL, CAPU + CAPI), split(jnp.concatenate(tails, axis=0))),
            )
        )

    def scatter(kind, base, size):
        total = None
        for source in kinds:
            req, scale, (hi, lo) = source[kind]
            hit = iota((size, req.shape[1]), 0) + base == req
            put = jnp.where(hit, scale, 0.0).astype(BF16)
            part = 256.0 * mm(put, hi) + mm(put, lo)
            total = part if total is None else total + part
        return total

    own_u, own_i, own_w = users_ref.shape[0], items_ref.shape[0], weeks_ref.shape[0]
    step = min(512, own_u)
    for c in range(0, own_u, step):
        dense_part = parts[0][c : c + step, :]
        for p in parts[1:]:
            dense_part = dense_part + p[c : c + step, :]
        users_ref[c : c + step, :] = dense_part + scatter(0, n * own_u + c, step)
    step = min(512, own_i)
    for c in range(0, own_i, step):
        items_ref[c : c + step, :] = scatter(1, n * own_i + c, step)
    weeks_ref[...] = scatter(2, n * own_w, own_w)


def owner_sums(n, gots, rets, parts, own_u, own_i, own_w):
    shares = len(gots)
    return pl.pallas_call(
        functools.partial(owner_kernel, shares),
        in_specs=[SM] + [VM] * (3 * shares),
        out_specs=[VM] * 3,
        out_shape=[jax.ShapeDtypeStruct((r, RANK), F32) for r in (own_u, own_i, own_w)],
        compiler_params=params(),
        cost_estimate=cost(6 << 30, 8 << 20),
        name="owner_sums",
    )(n, *gots, *rets, *parts)


def local(
    user_table,
    item_table,
    week_table,
    profile,
    feature_table,
    user_req,
    item_req,
    week_req,
    user_counts,
    item_counts,
    week_counts,
    pos_cells,
):
    owners = lax.axis_size("wide")
    shares = lax.axis_size("narrow")
    n = lax.axis_index("narrow").astype(I32).reshape(1)
    w = lax.axis_index("wide").astype(I32).reshape(1)

    def across(x):
        return lax.all_to_all(x, "wide", split_axis=0, concat_axis=0, tiled=True)

    def shift(x, r):
        return lax.ppermute(x, "narrow", [(i, (i + r) % shares) for i in range(shares)])

    spare = jnp.zeros((owners, 128 - CAPU - CAPI - CAPW), I32)
    got = across(jnp.concatenate([user_req[0], item_req[0], week_req[0], spare], axis=1))
    back = across(gather_rows(got, user_table, item_table, week_table))
    bits = positives(pos_cells[0])
    others, mine, packed = dense(n, profile, user_table, feature_table, shares)
    own_u = mine.shape[0]
    c = feature_table.shape[0] // 16
    shard_a, shard_b = sum_features(across(packed), c)
    grad_features = decode_features(w, spread(shard_a, ORDER_A), spread(shard_b, ORDER_B), c)
    ret = across(block_slots(back, bits, user_counts, item_counts, week_counts))
    gots = [got] + [shift(got, r) for r in range(1, shares)]
    rets = [ret] + [shift(ret, r) for r in range(1, shares)]
    parts = [mine] + [shift(others[own_u * (r - 1) : own_u * r], r) for r in range(1, shares)]
    grad_users, grad_items, grad_weeks = owner_sums(
        n, gots, rets, parts, own_u, item_table.shape[0] // shares, week_table.shape[0] // shares
    )
    return (grad_users, grad_items, grad_weeks, grad_features)


def solution(mesh):
    return jax.shard_map(
        local,
        mesh=mesh,
        in_specs=(
            P("wide", None),
            P("wide", None),
            P("wide", None),
            P("wide", "narrow"),
            P("narrow", None),
            P(("wide", "narrow"), None, None),
            P(("wide", "narrow"), None, None),
            P(("wide", "narrow"), None, None),
            P(("wide", "narrow"), None),
            P(("wide", "narrow"), None),
            P(("wide", "narrow"), None),
            P(("wide", "narrow"), None),
        ),
        out_specs=(
            P(("wide", "narrow"), None),
            P(("wide", "narrow"), None),
            P(("wide", "narrow"), None),
            P("narrow", None),
        ),
        check_vma=False,
    )
```

```python
import functools

import jax
import jax.numpy as jnp
from jax import lax
from jax.experimental import pallas as pl
from jax.experimental.pallas import tpu as pltpu
from jax.sharding import PartitionSpec as P

RANK = 256
BU = 256
BI = 256
BW = 28
BWP = 32
CAPU = 32
CAPI = 32
CAPW = 4
SLOT = 80
TAIL = 16
PLANE = 4
HALF = 14
F32, BF16, I32, I16 = jnp.float32, jnp.bfloat16, jnp.int32, jnp.int16
NN = (((1,), (0,)), ((), ()))
NT = (((1,), (1,)), ((), ()))
TN = (((0,), (0,)), ((), ()))


def mm(a, b, dims=NN):
    return lax.dot_general(a, b, dims, preferred_element_type=F32)


def iota(shape, dim):
    return lax.broadcasted_iota(I32, shape, dim)


def params(mib, **kw):
    return pltpu.CompilerParams(vmem_limit_bytes=mib << 20, **kw)


def cost(flops, nbytes):
    return pl.CostEstimate(flops=flops, bytes_accessed=nbytes, transcendentals=0)


def busy(us):
    return cost(us * 1_150_000_000, 0)


VM = pl.BlockSpec(memory_space=pltpu.VMEM)
SM = pl.BlockSpec(memory_space=pltpu.SMEM)


def pow2(e):
    return jnp.exp2(e).astype(BF16).astype(F32)


def row_exponent(g):
    m = jnp.max(jnp.abs(g), axis=1, keepdims=True)
    return jnp.clip(jnp.ceil(jnp.log2(jnp.maximum(m, 1e-30))), -96.0, 110.0)


def column_of(row):
    return jnp.broadcast_to(row, (128, 128)).T[:, :1]


def request_kernel(u_ref, v_ref, wt_ref, out_ref, flip):
    out_ref[...] = jnp.zeros_like(out_ref)
    out_ref[:, :CAPU] = u_ref[...]
    out_ref[:, CAPU : CAPU + CAPI] = v_ref[...]
    flip[...] = jnp.zeros_like(flip)
    flip[:CAPW, : wt_ref.shape[1]] = wt_ref[...]
    out_ref[:, CAPU + CAPI : CAPU + CAPI + CAPW] = flip[...].T[: out_ref.shape[0], :CAPW]


def requests(u, v, w):
    return pl.pallas_call(
        request_kernel,
        in_specs=[VM] * 3,
        out_specs=VM,
        out_shape=jax.ShapeDtypeStruct((u.shape[0], 128), I32),
        scratch_shapes=[pltpu.VMEM((128, 128), I32)],
        compiler_params=params(58),
        name="requests",
    )(u, v, w.T)


def gather_kernel(owners, got_ref, ut_ref, it_ref, wt_ref, out_ref):
    got = got_ref[...]
    flip = jnp.concatenate([got, jnp.zeros((128 - owners, 128), I32)], axis=0).T

    def pick(first, count, table_ref, step):
        col = jnp.concatenate([flip[first : first + count, w : w + 1] for w in range(owners)], axis=0)
        rows = table_ref.shape[0]
        acc = None
        for c in range(0, rows, step):
            hit = iota((owners * count, step), 1) == col - c
            part = mm(jnp.where(hit, 1.0, 0.0).astype(BF16), table_ref[c : c + step, :])
            acc = part if acc is None else acc + part
        return acc.astype(BF16)

    u = pick(0, CAPU, ut_ref, 512)
    v = pick(CAPU, CAPI, it_ref, 512)
    w = pick(CAPU + CAPI, TAIL, wt_ref, wt_ref.shape[0])
    for o in range(owners):
        b = SLOT * o
        out_ref[b : b + CAPU, :] = u[CAPU * o : CAPU * (o + 1)]
        out_ref[b + CAPU : b + CAPU + CAPI, :] = v[CAPI * o : CAPI * (o + 1)]
        out_ref[b + CAPU + CAPI : b + SLOT, :] = w[TAIL * o : TAIL * (o + 1)]


def gather_rows(got, ut, it, wt):
    owners = got.shape[0]
    return pl.pallas_call(
        functools.partial(gather_kernel, owners),
        in_specs=[VM] * 4,
        out_specs=VM,
        out_shape=jax.ShapeDtypeStruct((owners * SLOT, RANK), BF16),
        compiler_params=params(58),
        cost_estimate=busy(5),
        name="gather_rows",
    )(got, ut, it, wt)


def positives_kernel(p_ref, out_ref):
    n = p_ref.shape[0]
    rows = [p_ref[c : c + 1, :] for c in range(n)]
    near = [None] * n
    for a in range(n):
        col = jnp.broadcast_to(rows[a], (128, 128)).T
        for c in range(a, n):
            x = col ^ rows[c]
            if c == a:
                x = jnp.where(iota((128, 128), 0) < iota((128, 128), 1), x, 1)
            best = x[0:8]
            for s in range(8, 128, 8):
                best = jnp.minimum(best, x[s : s + 8])
            near[c] = best if near[c] is None else jnp.minimum(near[c], best)
    lo = hi = None
    group = 4
    for g in range(0, n, group):
        pos = jnp.concatenate(rows[g : g + group], axis=1)
        first = jnp.concatenate([jnp.min(near[c], axis=0, keepdims=True) for c in range(g, g + group)], axis=1)
        week = pos >> 16
        bit = jnp.where(first == 0, 0, 1)
        low = jnp.where(week < HALF, bit << week, 0).astype(F32)
        high = jnp.where(week < HALF, 0, bit << jnp.maximum(week - HALF, 0)).astype(F32)
        user_hit = iota((BU, group * 128), 0) == (pos >> 8) & (BU - 1)
        item_hit = iota((BI, group * 128), 0) == pos & (BI - 1)
        item = jnp.where(item_hit, 1.0, 0.0).astype(BF16)
        part_lo = mm(jnp.where(user_hit, low, 0.0).astype(BF16), item, NT)
        part_hi = mm(jnp.where(user_hit, high, 0.0).astype(BF16), item, NT)
        lo = part_lo if lo is None else lo + part_lo
        hi = part_hi if hi is None else hi + part_hi
    out_ref[...] = lo.astype(I32) | (hi.astype(I32) << HALF)


def positives(pos):
    return pl.pallas_call(
        positives_kernel,
        in_specs=[VM],
        out_specs=VM,
        out_shape=jax.ShapeDtypeStruct((BU, BI), I32),
        compiler_params=params(12),
        cost_estimate=busy(6),
        name="positives",
    )(pos.reshape(-1, 128))


def block_kernel(owners, back_ref, bits_ref, uc_ref, vc_ref, wc_ref, out_ref, gu, gvt, gw):
    def listed(count_ref, cap, stride, first, total):
        slots = owners * stride
        lane = iota((1, slots), 1)
        place = jnp.full((1, slots), -1, I32)
        start = 0
        back = []
        for o in range(owners):
            n = count_ref[0, o]
            s = lane - stride * o
            place = jnp.where((s >= 0) & (s < n), start + s, place)
            sub = iota((stride, total), 0)
            hit = (iota((stride, total), 1) == sub + start) & (sub < n)
            back.append(jnp.where(hit, 1.0, 0.0))
            start = start + n
        hit = iota((total, slots), 0) == place
        got = jnp.concatenate(
            [back_ref[SLOT * o + first : SLOT * o + first + stride, :] for o in range(owners)], axis=0
        )
        rows = mm(jnp.where(hit, 1.0, 0.0).astype(BF16), got)
        return rows, hit, jnp.concatenate(back, axis=0).astype(BF16)

    u, hit_u, into_u = listed(uc_ref, CAPU, CAPU, 0, BU)
    v, hit_v, into_v = listed(vc_ref, CAPI, CAPI, CAPU, BI)
    w, hit_w, into_w = listed(wc_ref, CAPW, TAIL, CAPU + CAPI, BWP)
    vb = v.astype(BF16)
    vt = v.T.astype(BF16)
    ut = u.T
    wt = jnp.concatenate([w, jnp.zeros((128 - BWP, RANK), F32)], axis=0).T
    gw[...] = jnp.zeros_like(gw)
    bits = bits_ref
    for k in range(BW):
        wk = w[k : k + 1, :]
        uw = (u * wk).astype(BF16)
        m = mm(uw, vt)
        pos = ((bits[...] >> k) & 1).astype(F32)
        g = (1.0 / (1.0 + jnp.exp(-m)) - pos).astype(BF16)
        q = mm(g, vb)
        uwt = (ut * wt[:, k : k + 1]).astype(BF16)
        pv = mm(uwt, g)
        if k == 0:
            gu[...] = q * wk
            gvt[...] = pv
        else:
            gu[...] += q * wk
            gvt[...] += pv
        gw[k : k + 1, :] = jnp.sum(q * u, axis=0, keepdims=True)

    def slots_of(g, hit, into):
        e = row_exponent(g)
        q = jnp.round(g * pow2(14.0 - e))
        hi = jnp.round(q * (1.0 / 256.0))
        lo = q - 256.0 * hi
        placed = 256.0 * mm(into, hi.astype(BF16)) + mm(into, lo.astype(BF16))
        row = jnp.sum(jnp.where(hit, e, 0.0), axis=0, keepdims=True)
        return placed, row

    qu, eu = slots_of(gu[...], hit_u, into_u)
    qv, ev = slots_of(gvt[...].T, hit_v, into_v)
    qw, ew = slots_of(gw[...], hit_w, into_w)
    lane = iota((8, 128), 1)

    def to_lane(row, width, o, lane_at):
        per = 128 // width
        cut = jnp.broadcast_to(row[:, 128 * (o // per) : 128 * (o // per + 1)], (8, 128))
        return pltpu.roll(cut, (lane_at - width * (o % per)) % 128, 1)

    sub = iota((TAIL, RANK), 0)
    for o in range(owners):
        b = SLOT * o
        out_ref[b : b + CAPU, :] = qu[CAPU * o : CAPU * (o + 1)].astype(I32).astype(I16)
        out_ref[b + CAPU : b + CAPU + CAPI, :] = qv[CAPI * o : CAPI * (o + 1)].astype(I32).astype(I16)
        exps = jnp.where(
            lane < CAPU,
            to_lane(eu, CAPU, o, 0),
            jnp.where(lane < CAPU + CAPI, to_lane(ev, CAPI, o, CAPU), to_lane(ew, TAIL, o, CAPU + CAPI)),
        )
        exps = jnp.concatenate([exps[0:1], exps[0:1]], axis=1)
        tail = jnp.where(sub == 8, exps, jnp.where(sub < CAPW, qw[TAIL * o : TAIL * (o + 1)], 0.0))
        out_ref[b + CAPU + CAPI : b + SLOT, :] = tail.astype(I32).astype(I16)


def block_slots(back, bits, uc, vc, wc):
    owners = uc.shape[1]
    return pl.pallas_call(
        functools.partial(block_kernel, owners),
        in_specs=[VM, VM, SM, SM, SM],
        out_specs=VM,
        out_shape=jax.ShapeDtypeStruct((owners * SLOT, RANK), I16),
        scratch_shapes=[pltpu.VMEM((BU, RANK), F32), pltpu.VMEM((RANK, BI), F32), pltpu.VMEM((BWP, RANK), F32)],
        compiler_params=params(20),
        cost_estimate=busy(30),
        name="block_slots",
    )(back, bits, uc, vc, wc)


def dense_kernel(shares, per, chunk, n_ref, w_ref, x_ref, u_ref, f_ref, others_ref, mine_ref, own_ref, g1, g2, g3, acc, ft):
    t = pl.program_id(0)
    u = u_ref[...]
    nf = f_ref.shape[0]

    @pl.when(t == 0)
    def _():
        acc[...] = jnp.zeros_like(acc)
        ft[...] = f_ref[...].astype(F32).T.astype(BF16)

    total = None
    for c in range(0, nf, chunk):
        f = f_ref[c : c + chunk, :]
        r = (mm(u, ft[:, c : c + chunk]) - x_ref[:, c : c + chunk].astype(F32)).astype(BF16)
        part = mm(r, f)
        total = part if total is None else total + part
        acc[c : c + chunk, :] += mm(r, u, TN)

    @pl.when(t < (shares - 1) * per)
    def _():
        others_ref[...] = 0.0625 * total

    @pl.when(t >= (shares - 1) * per)
    def _():
        mine_ref[...] = 0.0625 * total

    @pl.when(t == pl.num_programs(0) - 1)
    def _():
        share_out(acc, 0.0625, nf // PLANE, lax.rem(w_ref[0], PLANE), own_ref, (g1, g2, g3))


def share_out(ref, factor, r, me, own_ref, outs):
    def part(m):
        return factor * ref[pl.ds(pl.multiple_of((me ^ m) * r, r), r), :]

    own_ref[...] = part(0)
    for m in range(1, 4):
        pack(part(m), outs[m - 1], 0)


def pack(g, out_ref, base):
    r = g.shape[0]
    e = row_exponent(g)
    q = jnp.round(g * pow2(14.0 - e))
    out_ref[base : base + r, :] = q.astype(I32).astype(I16)
    tail = jnp.zeros((TAIL, RANK), F32)
    sub = iota((TAIL, RANK), 0)
    step = min(r, 128)
    eye = iota((step, 128), 0) == iota((step, 128), 1)
    for i in range(r // step):
        row = jnp.sum(jnp.where(eye, e[step * i : step * (i + 1)], 0.0), axis=0, keepdims=True)
        tail = jnp.where(sub == 8 + i, jnp.concatenate([row, row], axis=1), tail)
    out_ref[base + r : base + r + TAIL, :] = tail.astype(I32).astype(I16)


def unpack(ref, base, r):
    q = ref[base : base + r, :].astype(I32).astype(F32)
    tail = ref[base + r : base + r + TAIL, :].astype(I32).astype(F32)
    step = min(r, 128)
    e = [column_of(tail[8 + i : 9 + i, :128])[:step] for i in range(r // step)]
    return q * pow2(jnp.concatenate(e, axis=0) - 14.0)


def dense(n, w, x, u, f, shares):
    nu, nf = x.shape
    own = nu // shares
    tile = 512
    per = own // tile
    tiles = nu // tile

    def rows(t, n_ref, w_ref):
        return (lax.rem(n_ref[0] + 1 + t // per, shares) * per + lax.rem(t, per), 0)

    return pl.pallas_call(
        functools.partial(dense_kernel, shares, per, nf),
        grid_spec=pltpu.PrefetchScalarGridSpec(
            num_scalar_prefetch=2,
            grid=(tiles,),
            in_specs=[
                pl.BlockSpec((tile, nf), rows),
                pl.BlockSpec((tile, RANK), rows),
                pl.BlockSpec((nf, RANK), lambda t, n_ref, w_ref: (0, 0)),
            ],
            out_specs=[
                pl.BlockSpec((tile, RANK), lambda t, n_ref, w_ref: (jnp.minimum(t, (shares - 1) * per - 1), 0)),
                pl.BlockSpec((tile, RANK), lambda t, n_ref, w_ref: (jnp.maximum(t - (shares - 1) * per, 0), 0)),
                pl.BlockSpec((nf // PLANE, RANK), lambda t, n_ref, w_ref: (0, 0)),
            ]
            + [pl.BlockSpec((nf // PLANE + TAIL, RANK), lambda t, n_ref, w_ref: (0, 0))] * 3,
            scratch_shapes=[pltpu.VMEM((nf, RANK), F32), pltpu.VMEM((RANK, nf), BF16)],
        ),
        out_shape=[
            jax.ShapeDtypeStruct(((shares - 1) * own, RANK), F32),
            jax.ShapeDtypeStruct((own, RANK), F32),
            jax.ShapeDtypeStruct((nf // PLANE, RANK), F32),
        ]
        + [jax.ShapeDtypeStruct((nf // PLANE + TAIL, RANK), I16)] * 3,
        compiler_params=params(58, dimension_semantics=("arbitrary",)),
        cost_estimate=cost(3 * 2 * nu * nf * RANK, 2 * nu * nf + 8 * nu * RANK),
        name="dense",
    )(n, w, x, u, f)


def sum_kernel(r, w_ref, own_ref, in1, in2, in3, out_ref, g1, g2, g3, total):
    total[...] = (own_ref[...] + unpack(in1, 0, r)) + (unpack(in2, 0, r) + unpack(in3, 0, r))
    share_out(total, 1.0, r // 4, w_ref[0] // PLANE, out_ref, (g1, g2, g3))


def sum_plane(w, own, parts):
    r = own.shape[0]
    return pl.pallas_call(
        functools.partial(sum_kernel, r),
        in_specs=[SM] + [VM] * 4,
        out_specs=[VM] * 4,
        out_shape=[jax.ShapeDtypeStruct((r // 4, RANK), F32)]
        + [jax.ShapeDtypeStruct((r // 4 + TAIL, RANK), I16)] * 3,
        scratch_shapes=[pltpu.VMEM((r, RANK), F32)],
        compiler_params=params(12),
        cost_estimate=busy(25),
        name="sum_plane",
    )(w, own, *parts)


def last_kernel(c, own_ref, in1, in2, in3, out_ref):
    pack((own_ref[...] + unpack(in1, 0, c)) + (unpack(in2, 0, c) + unpack(in3, 0, c)), out_ref, 0)


def sum_line(own, parts):
    c = own.shape[0]
    return pl.pallas_call(
        functools.partial(last_kernel, c),
        in_specs=[VM] * 4,
        out_specs=VM,
        out_shape=jax.ShapeDtypeStruct((c + TAIL, RANK), I16),
        compiler_params=params(12),
        cost_estimate=busy(25),
        name="sum_line",
    )(own, *parts)


def decode_kernel(c, w_ref, *refs):
    out_ref = refs[-1]
    place, height = w_ref[0] % PLANE, w_ref[0] // PLANE
    for m in range(PLANE):
        for z in range(4):
            at = pl.multiple_of(((place ^ m) * 4 + (height ^ z)) * c, c)
            out_ref[pl.ds(at, c), :] = unpack(refs[m], (c + TAIL) * z, c)


def decode_features(w, parts, c):
    return pl.pallas_call(
        functools.partial(decode_kernel, c),
        in_specs=[SM] + [VM] * PLANE,
        out_specs=VM,
        out_shape=jax.ShapeDtypeStruct((16 * c, RANK), F32),
        compiler_params=params(12),
        cost_estimate=cost(1 << 20, 3 << 20),
        name="decode_features",
    )(w, *parts)


def lanes(x, width, off):
    per = 128 // width
    rolled = [pltpu.roll(x, (width * j - off) % 128, 1) for j in range(per)]
    lane = iota((1, 128), 1) // width
    out = []
    for g in range(16 // per):
        acc = rolled[0][per * g : per * g + 1, :]
        for j in range(1, per):
            acc = jnp.where(lane == j, rolled[j][per * g + j : per * g + j + 1, :], acc)
        out.append(acc)
    return jnp.concatenate(out, axis=1)


def owner_kernel(shares, n_ref, *refs):
    gots, rets = refs[:shares], refs[shares : 2 * shares]
    parts = refs[2 * shares : 3 * shares]
    users_ref, items_ref, weeks_ref = refs[3 * shares :]
    n = n_ref[0]
    kinds = []
    for got_ref, ret_ref in zip(gots, rets):
        got = got_ref[...]
        tails = [
            ret_ref[SLOT * o + CAPU + CAPI : SLOT * (o + 1), :].astype(I32).astype(F32) for o in range(16)
        ]
        exps = jnp.concatenate([t[8:9, :128] for t in tails], axis=0)
        scale = pow2(exps - 14.0)

        def split(q):
            hi = jnp.round(q * (1.0 / 256.0))
            return hi.astype(BF16), (q - 256.0 * hi).astype(BF16)

        def rows(first, count):
            return jnp.concatenate(
                [ret_ref[SLOT * o + first : SLOT * o + first + count, :] for o in range(16)], axis=0
            ).astype(I32).astype(F32)

        tail_ok = iota((1, 16 * TAIL), 1) % TAIL < CAPW
        wk = jnp.where(tail_ok, lanes(got, TAIL, CAPU + CAPI), -1)
        kinds.append(
            (
                (lanes(got, CAPU, 0), lanes(scale, CAPU, 0), split(rows(0, CAPU))),
                (lanes(got, CAPI, CAPU), lanes(scale, CAPI, CAPU), split(rows(CAPU, CAPI))),
                (wk, lanes(scale, TAIL, CAPU + CAPI), split(jnp.concatenate(tails, axis=0))),
            )
        )

    def scatter(kind, base, size):
        total = None
        for source in kinds:
            req, scale, (hi, lo) = source[kind]
            hit = iota((size, req.shape[1]), 0) + base == req
            put = jnp.where(hit, scale, 0.0).astype(BF16)
            part = 256.0 * mm(put, hi) + mm(put, lo)
            total = part if total is None else total + part
        return total

    own_u, own_i, own_w = users_ref.shape[0], items_ref.shape[0], weeks_ref.shape[0]
    step = min(512, own_u)
    for c in range(0, own_u, step):
        dense_part = parts[0][c : c + step, :]
        for p in parts[1:]:
            dense_part = dense_part + p[c : c + step, :]
        users_ref[c : c + step, :] = dense_part + scatter(0, n * own_u + c, step)
    step = min(512, own_i)
    for c in range(0, own_i, step):
        items_ref[c : c + step, :] = scatter(1, n * own_i + c, step)
    weeks_ref[...] = scatter(2, n * own_w, own_w)


def owner_sums(n, gots, rets, parts, own_u, own_i, own_w):
    shares = len(gots)
    return pl.pallas_call(
        functools.partial(owner_kernel, shares),
        in_specs=[SM] + [VM] * (3 * shares),
        out_specs=[VM] * 3,
        out_shape=[jax.ShapeDtypeStruct((r, RANK), F32) for r in (own_u, own_i, own_w)],
        compiler_params=params(28),
        cost_estimate=busy(30),
        name="owner_sums",
    )(n, *gots, *rets, *parts)


def local(
    user_table,
    item_table,
    week_table,
    profile,
    feature_table,
    user_req,
    item_req,
    week_req,
    user_counts,
    item_counts,
    week_counts,
    pos_cells,
):
    owners = lax.axis_size("wide")
    shares = lax.axis_size("narrow")
    n = lax.axis_index("narrow").astype(I32).reshape(1)
    w = lax.axis_index("wide").astype(I32).reshape(1)

    def flip(x, bits):
        return lax.ppermute(x, "wide", [(i, i ^ bits) for i in range(owners)])

    def across(x):
        return lax.all_to_all(x, "wide", split_axis=0, concat_axis=0, tiled=True)

    def shift(x, r):
        return lax.ppermute(x, "narrow", [(i, (i + r) % shares) for i in range(shares)])

    tie = lax.optimization_barrier
    got = across(requests(user_req[0], item_req[0], week_req[0]))
    bits = positives(pos_cells[0])
    got, bits = tie((got, bits))
    n, rows = tie((n, gather_rows(got, user_table, item_table, week_table)))
    back = across(rows)
    others, mine, own, *packed = dense(n, w, profile, user_table, feature_table, shares)
    own_u = mine.shape[0]
    back, own = tie((back, own))
    slots = block_slots(back, bits, user_counts, item_counts, week_counts)
    packed = [flip(x, m + 1) for m, x in enumerate(packed)]
    own, slots = tie((own, slots))
    own, *packed = sum_plane(w, own, packed)
    ret = across(slots)
    mark = sum_line(own, [flip(x, PLANE * (m + 1)) for m, x in enumerate(packed)])
    known = jnp.concatenate([mark] + [flip(mark, PLANE * m) for m in range(1, 4)], axis=0)
    ret, known = tie((ret, known))
    knowns = [known] + [flip(known, m) for m in range(1, PLANE)]
    gots = [got] + [shift(got, r) for r in range(1, shares)]
    rets = [ret] + [shift(ret, r) for r in range(1, shares)]
    parts = [mine] + [shift(others[own_u * (r - 1) : own_u * r], r) for r in range(1, shares)]
    grad_users, grad_items, grad_weeks = owner_sums(
        n, gots, rets, parts, own_u, item_table.shape[0] // shares, week_table.shape[0] // shares
    )
    w, grad_weeks = tie((w, grad_weeks))
    grad_features = decode_features(w, knowns, feature_table.shape[0] // owners)
    return (grad_users, grad_items, grad_weeks, grad_features)


def solution(mesh):
    return jax.shard_map(
        local,
        mesh=mesh,
        in_specs=(
            P("wide", None),
            P("wide", None),
            P("wide", None),
            P("wide", "narrow"),
            P("narrow", None),
            P(("wide", "narrow"), None, None),
            P(("wide", "narrow"), None, None),
            P(("wide", "narrow"), None, None),
            P(("wide", "narrow"), None),
            P(("wide", "narrow"), None),
            P(("wide", "narrow"), None),
            P(("wide", "narrow"), None),
        ),
        out_specs=(
            P(("wide", "narrow"), None),
            P(("wide", "narrow"), None),
            P(("wide", "narrow"), None),
            P("narrow", None),
        ),
        check_vma=False,
    )
```

```python
import functools

import jax
import jax.numpy as jnp
from jax import lax
from jax.experimental import pallas as pl
from jax.experimental.pallas import tpu as pltpu
from jax.sharding import PartitionSpec as P

RANK = 256
BU = 256
BI = 256
BW = 28
BWP = 32
CAPU = 32
CAPI = 32
CAPW = 4
SLOT = 80
TAIL = 16
PLANE = 4
HALF = 14
F32, BF16, I32, I16 = jnp.float32, jnp.bfloat16, jnp.int32, jnp.int16
NN = (((1,), (0,)), ((), ()))
NT = (((1,), (1,)), ((), ()))
TN = (((0,), (0,)), ((), ()))


def mm(a, b, dims=NN):
    return lax.dot_general(a, b, dims, preferred_element_type=F32)


def iota(shape, dim):
    return lax.broadcasted_iota(I32, shape, dim)


def params(mib, **kw):
    return pltpu.CompilerParams(vmem_limit_bytes=mib << 20, **kw)


def cost(flops, nbytes):
    return pl.CostEstimate(flops=flops, bytes_accessed=nbytes, transcendentals=0)


def busy(us):
    return cost(us * 1_150_000_000, 0)


VM = pl.BlockSpec(memory_space=pltpu.VMEM)
SM = pl.BlockSpec(memory_space=pltpu.SMEM)


def pow2(e):
    return jnp.exp2(e).astype(BF16).astype(F32)


def row_exponent(g):
    m = jnp.max(jnp.abs(g), axis=1, keepdims=True)
    return jnp.clip(jnp.ceil(jnp.log2(jnp.maximum(m, 1e-30))), -96.0, 110.0)


def column_of(row):
    return jnp.broadcast_to(row, (128, 128)).T[:, :1]


def request_kernel(u_ref, v_ref, wt_ref, out_ref, flip):
    out_ref[...] = jnp.zeros_like(out_ref)
    out_ref[:, :CAPU] = u_ref[...]
    out_ref[:, CAPU : CAPU + CAPI] = v_ref[...]
    flip[...] = jnp.zeros_like(flip)
    flip[:CAPW, : wt_ref.shape[1]] = wt_ref[...]
    out_ref[:, CAPU + CAPI : CAPU + CAPI + CAPW] = flip[...].T[: out_ref.shape[0], :CAPW]


def requests(u, v, w):
    return pl.pallas_call(
        request_kernel,
        in_specs=[VM] * 3,
        out_specs=VM,
        out_shape=jax.ShapeDtypeStruct((u.shape[0], 128), I32),
        scratch_shapes=[pltpu.VMEM((128, 128), I32)],
        compiler_params=params(58),
        name="requests",
    )(u, v, w.T)


def gather_kernel(owners, got_ref, ut_ref, it_ref, wt_ref, out_ref):
    got = got_ref[...]
    flip = jnp.concatenate([got, jnp.zeros((128 - owners, 128), I32)], axis=0).T

    def pick(first, count, table_ref, step):
        col = jnp.concatenate([flip[first : first + count, w : w + 1] for w in range(owners)], axis=0)
        rows = table_ref.shape[0]
        acc = None
        for c in range(0, rows, step):
            hit = iota((owners * count, step), 1) == col - c
            part = mm(jnp.where(hit, 1.0, 0.0).astype(BF16), table_ref[c : c + step, :])
            acc = part if acc is None else acc + part
        return acc.astype(BF16)

    u = pick(0, CAPU, ut_ref, 512)
    v = pick(CAPU, CAPI, it_ref, 512)
    w = pick(CAPU + CAPI, TAIL, wt_ref, wt_ref.shape[0])
    for o in range(owners):
        b = SLOT * o
        out_ref[b : b + CAPU, :] = u[CAPU * o : CAPU * (o + 1)]
        out_ref[b + CAPU : b + CAPU + CAPI, :] = v[CAPI * o : CAPI * (o + 1)]
        out_ref[b + CAPU + CAPI : b + SLOT, :] = w[TAIL * o : TAIL * (o + 1)]


def gather_rows(got, ut, it, wt):
    owners = got.shape[0]
    return pl.pallas_call(
        functools.partial(gather_kernel, owners),
        in_specs=[VM] * 4,
        out_specs=VM,
        out_shape=jax.ShapeDtypeStruct((owners * SLOT, RANK), BF16),
        compiler_params=params(58),
        cost_estimate=busy(5),
        name="gather_rows",
    )(got, ut, it, wt)


def positives_kernel(p_ref, out_ref):
    n = p_ref.shape[0]
    rows = [p_ref[c : c + 1, :] for c in range(n)]
    near = [None] * n
    for a in range(n):
        col = jnp.broadcast_to(rows[a], (128, 128)).T
        for c in range(a, n):
            x = col ^ rows[c]
            if c == a:
                x = jnp.where(iota((128, 128), 0) < iota((128, 128), 1), x, 1)
            best = x[0:8]
            for s in range(8, 128, 8):
                best = jnp.minimum(best, x[s : s + 8])
            near[c] = best if near[c] is None else jnp.minimum(near[c], best)
    lo = hi = None
    group = 4
    for g in range(0, n, group):
        pos = jnp.concatenate(rows[g : g + group], axis=1)
        first = jnp.concatenate([jnp.min(near[c], axis=0, keepdims=True) for c in range(g, g + group)], axis=1)
        week = pos >> 16
        bit = jnp.where(first == 0, 0, 1)
        low = jnp.where(week < HALF, bit << week, 0).astype(F32)
        high = jnp.where(week < HALF, 0, bit << jnp.maximum(week - HALF, 0)).astype(F32)
        user_hit = iota((BU, group * 128), 0) == (pos >> 8) & (BU - 1)
        item_hit = iota((BI, group * 128), 0) == pos & (BI - 1)
        item = jnp.where(item_hit, 1.0, 0.0).astype(BF16)
        part_lo = mm(jnp.where(user_hit, low, 0.0).astype(BF16), item, NT)
        part_hi = mm(jnp.where(user_hit, high, 0.0).astype(BF16), item, NT)
        lo = part_lo if lo is None else lo + part_lo
        hi = part_hi if hi is None else hi + part_hi
    out_ref[...] = lo.astype(I32) | (hi.astype(I32) << HALF)


def positives(pos):
    return pl.pallas_call(
        positives_kernel,
        in_specs=[VM],
        out_specs=VM,
        out_shape=jax.ShapeDtypeStruct((BU, BI), I32),
        compiler_params=params(12),
        cost_estimate=busy(6),
        name="positives",
    )(pos.reshape(-1, 128))


def block_kernel(owners, back_ref, bits_ref, uc_ref, vc_ref, wc_ref, out_ref, gu, gvt, gw):
    def listed(count_ref, cap, stride, first, total):
        slots = owners * stride
        lane = iota((1, slots), 1)
        place = jnp.full((1, slots), -1, I32)
        start = 0
        back = []
        for o in range(owners):
            n = count_ref[0, o]
            s = lane - stride * o
            place = jnp.where((s >= 0) & (s < n), start + s, place)
            sub = iota((stride, total), 0)
            hit = (iota((stride, total), 1) == sub + start) & (sub < n)
            back.append(jnp.where(hit, 1.0, 0.0))
            start = start + n
        hit = iota((total, slots), 0) == place
        got = jnp.concatenate(
            [back_ref[SLOT * o + first : SLOT * o + first + stride, :] for o in range(owners)], axis=0
        )
        rows = mm(jnp.where(hit, 1.0, 0.0).astype(BF16), got)
        return rows, hit, jnp.concatenate(back, axis=0).astype(BF16)

    u, hit_u, into_u = listed(uc_ref, CAPU, CAPU, 0, BU)
    v, hit_v, into_v = listed(vc_ref, CAPI, CAPI, CAPU, BI)
    w, hit_w, into_w = listed(wc_ref, CAPW, TAIL, CAPU + CAPI, BWP)
    vb = v.astype(BF16)
    vt = v.T.astype(BF16)
    ut = u.T
    wt = jnp.concatenate([w, jnp.zeros((128 - BWP, RANK), F32)], axis=0).T
    gw[...] = jnp.zeros_like(gw)
    bits = bits_ref
    for k in range(BW):
        wk = w[k : k + 1, :]
        uw = (u * wk).astype(BF16)
        m = mm(uw, vt)
        pos = ((bits[...] >> k) & 1).astype(F32)
        g = (1.0 / (1.0 + jnp.exp(-m)) - pos).astype(BF16)
        q = mm(g, vb)
        uwt = (ut * wt[:, k : k + 1]).astype(BF16)
        pv = mm(uwt, g)
        if k == 0:
            gu[...] = q * wk
            gvt[...] = pv
        else:
            gu[...] += q * wk
            gvt[...] += pv
        gw[k : k + 1, :] = jnp.sum(q * u, axis=0, keepdims=True)

    def slots_of(g, hit, into):
        e = row_exponent(g)
        q = jnp.round(g * pow2(14.0 - e))
        hi = jnp.round(q * (1.0 / 256.0))
        lo = q - 256.0 * hi
        placed = 256.0 * mm(into, hi.astype(BF16)) + mm(into, lo.astype(BF16))
        row = jnp.sum(jnp.where(hit, e, 0.0), axis=0, keepdims=True)
        return placed, row

    qu, eu = slots_of(gu[...], hit_u, into_u)
    qv, ev = slots_of(gvt[...].T, hit_v, into_v)
    qw, ew = slots_of(gw[...], hit_w, into_w)
    lane = iota((8, 128), 1)

    def to_lane(row, width, o, lane_at):
        per = 128 // width
        cut = jnp.broadcast_to(row[:, 128 * (o // per) : 128 * (o // per + 1)], (8, 128))
        return pltpu.roll(cut, (lane_at - width * (o % per)) % 128, 1)

    sub = iota((TAIL, RANK), 0)
    for o in range(owners):
        b = SLOT * o
        out_ref[b : b + CAPU, :] = qu[CAPU * o : CAPU * (o + 1)].astype(I32).astype(I16)
        out_ref[b + CAPU : b + CAPU + CAPI, :] = qv[CAPI * o : CAPI * (o + 1)].astype(I32).astype(I16)
        exps = jnp.where(
            lane < CAPU,
            to_lane(eu, CAPU, o, 0),
            jnp.where(lane < CAPU + CAPI, to_lane(ev, CAPI, o, CAPU), to_lane(ew, TAIL, o, CAPU + CAPI)),
        )
        exps = jnp.concatenate([exps[0:1], exps[0:1]], axis=1)
        tail = jnp.where(sub == 8, exps, jnp.where(sub < CAPW, qw[TAIL * o : TAIL * (o + 1)], 0.0))
        out_ref[b + CAPU + CAPI : b + SLOT, :] = tail.astype(I32).astype(I16)


def block_slots(back, bits, uc, vc, wc):
    owners = uc.shape[1]
    return pl.pallas_call(
        functools.partial(block_kernel, owners),
        in_specs=[VM, VM, SM, SM, SM],
        out_specs=VM,
        out_shape=jax.ShapeDtypeStruct((owners * SLOT, RANK), I16),
        scratch_shapes=[pltpu.VMEM((BU, RANK), F32), pltpu.VMEM((RANK, BI), F32), pltpu.VMEM((BWP, RANK), F32)],
        compiler_params=params(20),
        cost_estimate=busy(30),
        name="block_slots",
    )(back, bits, uc, vc, wc)


def dense_kernel(shares, per, chunk, n_ref, w_ref, x_ref, u_ref, f_ref, others_ref, mine_ref, own_ref, g1, g2, g3, acc):
    t = pl.program_id(0)
    u = u_ref[...]
    nf = f_ref.shape[0]

    @pl.when(t == 0)
    def _():
        acc[...] = jnp.zeros_like(acc)

    total = None
    for c in range(0, nf, chunk):
        f = f_ref[c : c + chunk, :]
        r = (mm(u, f, NT) - x_ref[:, c : c + chunk].astype(F32)).astype(BF16)
        part = mm(r, f)
        total = part if total is None else total + part
        acc[c : c + chunk, :] += mm(r, u, TN)

    @pl.when(t < (shares - 1) * per)
    def _():
        others_ref[...] = 0.0625 * total

    @pl.when(t >= (shares - 1) * per)
    def _():
        mine_ref[...] = 0.0625 * total

    @pl.when(t == pl.num_programs(0) - 1)
    def _():
        share_out(acc, 0.0625, nf // PLANE, lax.rem(w_ref[0], PLANE), own_ref, (g1, g2, g3))


def share_out(ref, factor, r, me, own_ref, outs):
    def part(m):
        return factor * ref[pl.ds(pl.multiple_of((me ^ m) * r, r), r), :]

    own_ref[...] = part(0)
    for m in range(1, 4):
        pack(part(m), outs[m - 1], 0)


def pack(g, out_ref, base):
    r = g.shape[0]
    e = row_exponent(g)
    q = jnp.round(g * pow2(14.0 - e))
    out_ref[base : base + r, :] = q.astype(I32).astype(I16)
    tail = jnp.zeros((TAIL, RANK), F32)
    sub = iota((TAIL, RANK), 0)
    step = min(r, 128)
    eye = iota((step, 128), 0) == iota((step, 128), 1)
    for i in range(r // step):
        row = jnp.sum(jnp.where(eye, e[step * i : step * (i + 1)], 0.0), axis=0, keepdims=True)
        tail = jnp.where(sub == 8 + i, jnp.concatenate([row, row], axis=1), tail)
    out_ref[base + r : base + r + TAIL, :] = tail.astype(I32).astype(I16)


def unpack(ref, base, r):
    q = ref[base : base + r, :].astype(I32).astype(F32)
    tail = ref[base + r : base + r + TAIL, :].astype(I32).astype(F32)
    step = min(r, 128)
    e = [column_of(tail[8 + i : 9 + i, :128])[:step] for i in range(r // step)]
    return q * pow2(jnp.concatenate(e, axis=0) - 14.0)


def dense(n, w, x, u, f, shares):
    nu, nf = x.shape
    own = nu // shares
    tile = 512
    per = own // tile
    tiles = nu // tile

    def rows(t, n_ref, w_ref):
        return (lax.rem(n_ref[0] + 1 + t // per, shares) * per + lax.rem(t, per), 0)

    return pl.pallas_call(
        functools.partial(dense_kernel, shares, per, nf),
        grid_spec=pltpu.PrefetchScalarGridSpec(
            num_scalar_prefetch=2,
            grid=(tiles,),
            in_specs=[
                pl.BlockSpec((tile, nf), rows),
                pl.BlockSpec((tile, RANK), rows),
                pl.BlockSpec((nf, RANK), lambda t, n_ref, w_ref: (0, 0)),
            ],
            out_specs=[
                pl.BlockSpec((tile, RANK), lambda t, n_ref, w_ref: (jnp.minimum(t, (shares - 1) * per - 1), 0)),
                pl.BlockSpec((tile, RANK), lambda t, n_ref, w_ref: (jnp.maximum(t - (shares - 1) * per, 0), 0)),
                pl.BlockSpec((nf // PLANE, RANK), lambda t, n_ref, w_ref: (0, 0)),
            ]
            + [pl.BlockSpec((nf // PLANE + TAIL, RANK), lambda t, n_ref, w_ref: (0, 0))] * 3,
            scratch_shapes=[pltpu.VMEM((nf, RANK), F32)],
        ),
        out_shape=[
            jax.ShapeDtypeStruct(((shares - 1) * own, RANK), F32),
            jax.ShapeDtypeStruct((own, RANK), F32),
            jax.ShapeDtypeStruct((nf // PLANE, RANK), F32),
        ]
        + [jax.ShapeDtypeStruct((nf // PLANE + TAIL, RANK), I16)] * 3,
        compiler_params=params(58, dimension_semantics=("arbitrary",)),
        cost_estimate=cost(3 * 2 * nu * nf * RANK, 2 * nu * nf + 8 * nu * RANK),
        name="dense",
    )(n, w, x, u, f)


def sum_kernel(r, w_ref, own_ref, in1, in2, in3, out_ref, g1, g2, g3, total):
    total[...] = (own_ref[...] + unpack(in1, 0, r)) + (unpack(in2, 0, r) + unpack(in3, 0, r))
    share_out(total, 1.0, r // 4, w_ref[0] // PLANE, out_ref, (g1, g2, g3))


def sum_plane(w, own, parts):
    r = own.shape[0]
    return pl.pallas_call(
        functools.partial(sum_kernel, r),
        in_specs=[SM] + [VM] * 4,
        out_specs=[VM] * 4,
        out_shape=[jax.ShapeDtypeStruct((r // 4, RANK), F32)]
        + [jax.ShapeDtypeStruct((r // 4 + TAIL, RANK), I16)] * 3,
        scratch_shapes=[pltpu.VMEM((r, RANK), F32)],
        compiler_params=params(12),
        cost_estimate=busy(25),
        name="sum_plane",
    )(w, own, *parts)


def last_kernel(c, own_ref, in1, in2, in3, out_ref):
    pack((own_ref[...] + unpack(in1, 0, c)) + (unpack(in2, 0, c) + unpack(in3, 0, c)), out_ref, 0)


def sum_line(own, parts):
    c = own.shape[0]
    return pl.pallas_call(
        functools.partial(last_kernel, c),
        in_specs=[VM] * 4,
        out_specs=VM,
        out_shape=jax.ShapeDtypeStruct((c + TAIL, RANK), I16),
        compiler_params=params(12),
        cost_estimate=busy(25),
        name="sum_line",
    )(own, *parts)


def decode_kernel(c, w_ref, *refs):
    out_ref = refs[-1]
    place, height = w_ref[0] % PLANE, w_ref[0] // PLANE
    for m in range(PLANE):
        for z in range(4):
            at = pl.multiple_of(((place ^ m) * 4 + (height ^ z)) * c, c)
            out_ref[pl.ds(at, c), :] = unpack(refs[m], (c + TAIL) * z, c)


def decode_features(w, parts, c):
    return pl.pallas_call(
        functools.partial(decode_kernel, c),
        in_specs=[SM] + [VM] * PLANE,
        out_specs=VM,
        out_shape=jax.ShapeDtypeStruct((16 * c, RANK), F32),
        compiler_params=params(12),
        cost_estimate=cost(1 << 20, 3 << 20),
        name="decode_features",
    )(w, *parts)


def lanes(x, width, off):
    per = 128 // width
    rolled = [pltpu.roll(x, (width * j - off) % 128, 1) for j in range(per)]
    lane = iota((1, 128), 1) // width
    out = []
    for g in range(16 // per):
        acc = rolled[0][per * g : per * g + 1, :]
        for j in range(1, per):
            acc = jnp.where(lane == j, rolled[j][per * g + j : per * g + j + 1, :], acc)
        out.append(acc)
    return jnp.concatenate(out, axis=1)


def owner_kernel(shares, n_ref, *refs):
    gots, rets = refs[:shares], refs[shares : 2 * shares]
    parts = refs[2 * shares : 3 * shares]
    users_ref, items_ref, weeks_ref = refs[3 * shares :]
    n = n_ref[0]
    kinds = []
    for got_ref, ret_ref in zip(gots, rets):
        got = got_ref[...]
        tails = [
            ret_ref[SLOT * o + CAPU + CAPI : SLOT * (o + 1), :].astype(I32).astype(F32) for o in range(16)
        ]
        exps = jnp.concatenate([t[8:9, :128] for t in tails], axis=0)
        scale = pow2(exps - 14.0)

        def split(q):
            hi = jnp.round(q * (1.0 / 256.0))
            return hi.astype(BF16), (q - 256.0 * hi).astype(BF16)

        def rows(first, count):
            return jnp.concatenate(
                [ret_ref[SLOT * o + first : SLOT * o + first + count, :] for o in range(16)], axis=0
            ).astype(I32).astype(F32)

        tail_ok = iota((1, 16 * TAIL), 1) % TAIL < CAPW
        wk = jnp.where(tail_ok, lanes(got, TAIL, CAPU + CAPI), -1)
        kinds.append(
            (
                (lanes(got, CAPU, 0), lanes(scale, CAPU, 0), split(rows(0, CAPU))),
                (lanes(got, CAPI, CAPU), lanes(scale, CAPI, CAPU), split(rows(CAPU, CAPI))),
                (wk, lanes(scale, TAIL, CAPU + CAPI), split(jnp.concatenate(tails, axis=0))),
            )
        )

    def scatter(kind, base, size):
        total = None
        for source in kinds:
            req, scale, (hi, lo) = source[kind]
            hit = iota((size, req.shape[1]), 0) + base == req
            put = jnp.where(hit, scale, 0.0).astype(BF16)
            part = 256.0 * mm(put, hi) + mm(put, lo)
            total = part if total is None else total + part
        return total

    own_u, own_i, own_w = users_ref.shape[0], items_ref.shape[0], weeks_ref.shape[0]
    step = min(512, own_u)
    for c in range(0, own_u, step):
        dense_part = parts[0][c : c + step, :]
        for p in parts[1:]:
            dense_part = dense_part + p[c : c + step, :]
        users_ref[c : c + step, :] = dense_part + scatter(0, n * own_u + c, step)
    step = min(512, own_i)
    for c in range(0, own_i, step):
        items_ref[c : c + step, :] = scatter(1, n * own_i + c, step)
    weeks_ref[...] = scatter(2, n * own_w, own_w)


def owner_sums(n, gots, rets, parts, own_u, own_i, own_w):
    shares = len(gots)
    return pl.pallas_call(
        functools.partial(owner_kernel, shares),
        in_specs=[SM] + [VM] * (3 * shares),
        out_specs=[VM] * 3,
        out_shape=[jax.ShapeDtypeStruct((r, RANK), F32) for r in (own_u, own_i, own_w)],
        compiler_params=params(28),
        cost_estimate=busy(1),
        name="owner_sums",
    )(n, *gots, *rets, *parts)


def local(
    user_table,
    item_table,
    week_table,
    profile,
    feature_table,
    user_req,
    item_req,
    week_req,
    user_counts,
    item_counts,
    week_counts,
    pos_cells,
):
    owners = lax.axis_size("wide")
    shares = lax.axis_size("narrow")
    n = lax.axis_index("narrow").astype(I32).reshape(1)
    w = lax.axis_index("wide").astype(I32).reshape(1)

    def flip(x, bits):
        return lax.ppermute(x, "wide", [(i, i ^ bits) for i in range(owners)])

    def across(x):
        return lax.all_to_all(x, "wide", split_axis=0, concat_axis=0, tiled=True)

    def shift(x, r):
        return lax.ppermute(x, "narrow", [(i, (i + r) % shares) for i in range(shares)])

    tie = lax.optimization_barrier
    got = across(requests(user_req[0], item_req[0], week_req[0]))
    bits = positives(pos_cells[0])
    got, bits = tie((got, bits))
    n, rows = tie((n, gather_rows(got, user_table, item_table, week_table)))
    back = across(rows)
    others, mine, own, *packed = dense(n, w, profile, user_table, feature_table, shares)
    own_u = mine.shape[0]
    back, own = tie((back, own))
    slots = block_slots(back, bits, user_counts, item_counts, week_counts)
    packed = [flip(x, m + 1) for m, x in enumerate(packed)]
    own, slots = tie((own, slots))
    own, *packed = sum_plane(w, own, packed)
    mark = sum_line(own, [flip(x, PLANE * (m + 1)) for m, x in enumerate(packed)])
    known = jnp.concatenate([mark] + [flip(mark, PLANE * m) for m in range(1, 4)], axis=0)
    slots, known = tie((slots, known))
    knowns = [known] + [flip(known, m) for m in range(1, PLANE)]
    ret = across(slots)
    ret, knowns[1], knowns[2] = tie((ret, knowns[1], knowns[2]))
    gots = [got] + [shift(got, r) for r in range(1, shares)]
    rets = [ret] + [shift(ret, r) for r in range(1, shares)]
    parts = [mine] + [shift(others[own_u * (r - 1) : own_u * r], r) for r in range(1, shares)]
    grad_users, grad_items, grad_weeks = owner_sums(
        n, gots, rets, parts, own_u, item_table.shape[0] // shares, week_table.shape[0] // shares
    )
    w, grad_weeks = tie((w, grad_weeks))
    grad_features = decode_features(w, knowns, feature_table.shape[0] // owners)
    return (grad_users, grad_items, grad_weeks, grad_features)


def solution(mesh):
    return jax.shard_map(
        local,
        mesh=mesh,
        in_specs=(
            P("wide", None),
            P("wide", None),
            P("wide", None),
            P("wide", "narrow"),
            P("narrow", None),
            P(("wide", "narrow"), None, None),
            P(("wide", "narrow"), None, None),
            P(("wide", "narrow"), None, None),
            P(("wide", "narrow"), None),
            P(("wide", "narrow"), None),
            P(("wide", "narrow"), None),
            P(("wide", "narrow"), None),
        ),
        out_specs=(
            P(("wide", "narrow"), None),
            P(("wide", "narrow"), None),
            P(("wide", "narrow"), None),
            P("narrow", None),
        ),
        check_vma=False,
    )
```
